32 devices in a mesh: rows: 16 (over z, x, core), snap: 2 (over y).
Axes of the slice: x: 2, y: 2, z: 4, core: 2. Of those that a mesh axis runs over, the one named last changes fastest.
Arguments:
- primal: float32 [16384, 1024], P('rows', 'snap'), may hold values from -6 to 6
- adjoint: float32 [16384, 1024], P('rows', 'snap'), may hold values from -6 to 6
- right_vectors: float32 [1024, 1024], P(None, 'snap'), may hold values from -0.1875 to 0.1875
- left_vectors: float32 [1024, 1024], P(None, 'snap'), may hold values from -0.1875 to 0.1875
- singular: float32 [1024], P('snap'), may hold values from 0.1 to 10
Outputs:
- gram: float32 [1024, 1024], P('rows', 'snap')
- phi_modes: float32 [16384, 1024], P('rows', 'snap')
- psi_modes: float32 [16384, 1024], P('rows', 'snap')
The draws below stay inside these ranges and needn't reach their ends.
All inputs are finite; a program needn't handle non-finite values.
Results may differ from the reference program's by a relative error of at most 0.00008.
Values sent between devices are 32-bit elements; how exact they have to be, the bound alone decides.
No kernel may reach another device: no remote copies, remote signals or barrier semaphores. Data moves between devices by JAX's collectives and lax.ppermute only.
A program may use at most 64 MiB of HBM per device.

```python
import math
import jax
import jax.numpy as jnp
from jax import lax

K = 1024
R = 1024
M = 16384


def shard_levels(key, extent, shards, low, high):
    gain, own = 1.0, jax.random.fold_in(key, 6)
    for dim, parts in shards:
        heights = jnp.exp(jax.random.uniform(jax.random.fold_in(own, dim), (parts,), jnp.float32, low / len(shards), high / len(shards)))
        gain = gain * jnp.repeat(heights, extent[dim] // parts).reshape([-1 if axis == dim else 1 for axis in range(len(extent))])
    return gain


def centred(rng, dims, spread, bound, shards=(), held_as=jnp.bfloat16):
    array = spread * jax.random.normal(rng, dims, jnp.float32)
    if shards:
        array = array * shard_levels(rng, dims, shards, -0.22, 0.18)
    return jnp.clip(array, -bound, bound).astype(held_as)


def setup_inputs(seed: int = 0) -> dict:
    streams_of = jax.random.split(jax.random.key(seed), 6)
    primal = centred(streams_of[0], (M, K), 1.0, 6.0, ((0, 16), (1, 2)), jnp.float32)
    adjoint = centred(streams_of[1], (M, K), 1.0, 6.0, ((0, 16), (1, 2)), jnp.float32)
    right_vectors = centred(streams_of[2], (K, R), K ** -0.5, 0.1875, ((1, 2),), jnp.float32)
    left_vectors = centred(streams_of[3], (K, R), K ** -0.5, 0.1875, ((1, 2),), jnp.float32)
    singular = jnp.clip(jnp.exp(math.log(10.0) - 4.6051702 * jax.random.uniform(streams_of[4], (R,), jnp.float32) ** shard_levels(streams_of[4], (R,), ((0, 2),), -0.2, 0.2)), 0.1, 10.0)
    return dict(primal=primal, adjoint=adjoint, right_vectors=right_vectors, left_vectors=left_vectors, singular=singular)


def reference(primal, adjoint, right_vectors, left_vectors, singular):
    norm = 1.0 / jnp.sqrt(jnp.float32(M))
    gram = lax.dot_general(adjoint, primal, (((0,), (0,)), ((), ())), precision=lax.Precision.HIGHEST, preferred_element_type=jnp.float32) * norm
    weights = 1.0 / jnp.sqrt(singular)
    phi_modes = jnp.dot(primal, right_vectors, precision=lax.Precision.HIGHEST, preferred_element_type=jnp.float32) * weights
    psi_modes = jnp.dot(adjoint, left_vectors, precision=lax.Precision.HIGHEST, preferred_element_type=jnp.float32) * weights
    return (gram, phi_modes, psi_modes)
```

```python
import functools

import jax
import jax.numpy as jnp
from jax import lax
from jax.experimental import pallas as pl
from jax.experimental.pallas import tpu as pltpu
from jax.sharding import PartitionSpec as P

HIGH = lax.Precision.HIGH


def mul(left, right):
    return jnp.dot(left, right, precision=HIGH, preferred_element_type=jnp.float32)


def split(x):
    high = x.astype(jnp.bfloat16)
    return high, (x - high.astype(jnp.float32)).astype(jnp.bfloat16)


def split_kernel(x_ref, high_ref, low_ref):
    high_ref[...], low_ref[...] = split(x_ref[...])


FREE = pl.CostEstimate(flops=0, bytes_accessed=0, transcendentals=0)


def split_matrix(matrix):
    return pl.pallas_call(
        split_kernel,
        out_shape=[jax.ShapeDtypeStruct(matrix.shape, jnp.bfloat16)] * 2,
        cost_estimate=FREE,
    )(matrix)


def inner_cols(left, right):
    return lax.dot_general(
        left, right, (((0,), (0,)), ((), ())), precision=HIGH, preferred_element_type=jnp.float32
    )


def add_rows_kernel(last, total_ref, x_ref, high_ref, low_ref, weights_ref, out_ref):
    dot = functools.partial(jnp.dot, preferred_element_type=jnp.float32)
    x_high, x_low = split(x_ref[...])
    total = total_ref[...] + (
        dot(x_high, high_ref[...]) + (dot(x_high, low_ref[...]) + dot(x_low, high_ref[...]))
    )
    out_ref[...] = total * weights_ref[...] if last else total


def add_rows(total, x, matrix, weights, start, tile, last):
    width = total.shape[1]
    depth = x.shape[1]
    first = start // tile
    rows = pl.BlockSpec((tile, width), lambda i: (first + i, 0))
    whole = pl.BlockSpec((depth, width), lambda i: (0, 0))
    return pl.pallas_call(
        functools.partial(add_rows_kernel, last),
        grid=(x.shape[0] // tile,),
        in_specs=[
            rows,
            pl.BlockSpec((tile, depth), lambda i: (i, 0)),
            whole,
            whole,
            pl.BlockSpec((1, width), lambda i: (0, 0)),
        ],
        out_specs=rows,
        out_shape=jax.ShapeDtypeStruct(total.shape, total.dtype),
        input_output_aliases={0: 0},
        cost_estimate=FREE,
    )(total, x, *matrix, weights[None])


def exchange(parts, axis, stride):
    count = lax.axis_size("rows")
    digits = parts.shape[axis]
    mine = (lax.axis_index("rows") // stride) % digits
    total = lax.dynamic_index_in_dim(parts, mine, axis, keepdims=False)
    for flip in range(1, digits):
        give = lax.dynamic_index_in_dim(parts, mine ^ flip, axis, keepdims=False)
        total += lax.ppermute(give, "rows", [(i, i ^ (flip * stride)) for i in range(count)])
    return total


def shards(primal, adjoint, right_vectors, left_vectors, singular):
    count = lax.axis_size("rows")
    sides = lax.axis_size("snap")
    side = lax.axis_index("snap")
    rows, width = primal.shape
    weights = 1.0 / jnp.sqrt(singular)
    norm = 1.0 / jnp.sqrt(jnp.float32(rows * count))
    ring = [(i, (i + 1) % sides) for i in range(sides)]
    cuts = [0, rows * 7 // 8, rows]
    spans = list(zip(cuts[:-1], cuts[1:]))

    def block(matrix, owner):
        return lax.dynamic_slice_in_dim(matrix, owner * width, width, 0)

    group = count // sides
    share = width // group

    near = min(group, 1 << (count.bit_length() - 1) // 2)

    def within(term):
        return exchange(term.reshape(group // near, near, share, width), 1, 1)

    adjoints = [adjoint]
    primals = [[primal[a:b] for a, b in spans]]
    for step in range(1, sides):
        adjoints.append(lax.ppermute(adjoints[-1], "snap", ring))
        primals.append([lax.ppermute(piece, "snap", ring) for piece in primals[-1]])

    terms = [within(inner_cols(adjoint, primal))]
    psi = mul(adjoint, block(left_vectors, side))
    phi = mul(primal, block(right_vectors, side))
    rights = []
    for step in range(1, sides):
        owner = (side - step) % sides
        left = split_matrix(block(left_vectors, owner))
        rights.append(split_matrix(block(right_vectors, owner)))
        theirs, left, rights, terms, psi, phi = lax.optimization_barrier(
            (adjoints[step], left, rights, terms, psi, phi)
        )
        terms.append(within(inner_cols(theirs, primal)))
        psi = add_rows(psi, theirs, left, weights, 0, rows // 2, step == sides - 1)
    blocks = [terms[-t % sides] for t in range(sides)]
    bit = 1
    while bit < sides:
        turn = (side // bit) % 2 == 1
        blocks = [jnp.where(turn, blocks[t - bit], blocks[t]) for t in range(sides)]
        bit *= 2
    total = exchange(jnp.concatenate(blocks), 0, near)
    gram = total * norm
    gram, psi, phi = lax.optimization_barrier((gram, psi, phi))
    for step in range(1, sides):
        for (start, stop), piece in zip(spans, primals[step]):
            tile = (stop - start) // (1 if start else 2)
            phi = add_rows(phi, piece, rights[step - 1], weights, start, tile, step == sides - 1)
    return (gram, phi, psi)


def solution(mesh):
    in_specs = (P("rows", "snap"), P("rows", "snap"), P(None, "snap"), P(None, "snap"), P("snap"))
    out_specs = (P("rows", "snap"), P("rows", "snap"), P("rows", "snap"))
    return jax.shard_map(shards, mesh=mesh, in_specs=in_specs, out_specs=out_specs, check_vma=False)
```

```python
import functools

import jax
import jax.numpy as jnp
from jax import lax
from jax.experimental import pallas as pl
from jax.experimental.pallas import tpu as pltpu
from jax.sharding import PartitionSpec as P

HIGH = lax.Precision.HIGH


def mul(left, right):
    return jnp.dot(left, right, precision=HIGH, preferred_element_type=jnp.float32)


def split(x):
    high = x.astype(jnp.bfloat16)
    return high, (x - high.astype(jnp.float32)).astype(jnp.bfloat16)


def split_kernel(x_ref, high_ref, low_ref):
    high_ref[...], low_ref[...] = split(x_ref[...])


LIMIT = 16 << 20
FREE = pl.CostEstimate(flops=0, bytes_accessed=0, transcendentals=0)


def split_matrix(matrix):
    return pl.pallas_call(
        split_kernel,
        out_shape=[jax.ShapeDtypeStruct(matrix.shape, jnp.bfloat16)] * 2,
        cost_estimate=FREE,
        compiler_params=pltpu.CompilerParams(vmem_limit_bytes=LIMIT),
    )(matrix)


def inner_cols(left, right):
    return lax.dot_general(
        left, right, (((0,), (0,)), ((), ())), precision=HIGH, preferred_element_type=jnp.float32
    )


def add_rows_kernel(last, total_ref, x_ref, high_ref, low_ref, weights_ref, out_ref):
    dot = functools.partial(jnp.dot, preferred_element_type=jnp.float32)
    x_high, x_low = split(x_ref[...])
    total = total_ref[...] + (
        dot(x_high, high_ref[...]) + (dot(x_high, low_ref[...]) + dot(x_low, high_ref[...]))
    )
    out_ref[...] = total * weights_ref[...] if last else total


def add_rows(total, x, matrix, weights, start, tile, last):
    width = total.shape[1]
    depth = x.shape[1]
    first = start // tile
    rows = pl.BlockSpec((tile, width), lambda i: (first + i, 0))
    whole = pl.BlockSpec((depth, width), lambda i: (0, 0))
    return pl.pallas_call(
        functools.partial(add_rows_kernel, last),
        grid=(x.shape[0] // tile,),
        in_specs=[
            rows,
            pl.BlockSpec((tile, depth), lambda i: (i, 0)),
            whole,
            whole,
            pl.BlockSpec((1, width), lambda i: (0, 0)),
        ],
        out_specs=rows,
        out_shape=jax.ShapeDtypeStruct(total.shape, total.dtype),
        input_output_aliases={0: 0},
        cost_estimate=FREE,
        compiler_params=pltpu.CompilerParams(vmem_limit_bytes=LIMIT),
    )(total, x, *matrix, weights[None])


def end_rows_kernel(first, last, total_ref, x_ref, high_ref, low_ref, weights_ref, out_ref, held, sems):
    rows = x_ref.shape[0]
    fetch = pltpu.make_async_copy(total_ref.at[pl.ds(first, rows)], held, sems.at[0])
    fetch.start()
    dot = functools.partial(jnp.dot, preferred_element_type=jnp.float32)
    x_high, x_low = split(x_ref[...])
    term = dot(x_high, high_ref[...]) + (dot(x_high, low_ref[...]) + dot(x_low, high_ref[...]))
    fetch.wait()
    total = held[...] + term
    held[...] = total * weights_ref[...] if last else total
    store = pltpu.make_async_copy(held, out_ref.at[pl.ds(first, rows)], sems.at[1])
    store.start()
    store.wait()


def end_rows(total, x, matrix, weights, start, last):
    vmem = pl.BlockSpec(memory_space=pltpu.VMEM)
    apart = pl.BlockSpec(memory_space=pl.ANY)
    return pl.pallas_call(
        functools.partial(end_rows_kernel, start, last),
        in_specs=[apart, vmem, vmem, vmem, vmem],
        out_specs=apart,
        out_shape=jax.ShapeDtypeStruct(total.shape, total.dtype),
        scratch_shapes=[
            pltpu.VMEM((x.shape[0], total.shape[1]), jnp.float32),
            pltpu.SemaphoreType.DMA((2,)),
        ],
        input_output_aliases={0: 0},
        cost_estimate=FREE,
        compiler_params=pltpu.CompilerParams(vmem_limit_bytes=LIMIT),
    )(total, x, *matrix, weights[None])


def exchange(parts, axis, stride):
    count = lax.axis_size("rows")
    digits = parts.shape[axis]
    mine = (lax.axis_index("rows") // stride) % digits
    total = lax.dynamic_index_in_dim(parts, mine, axis, keepdims=False)
    for flip in range(1, digits):
        give = lax.dynamic_index_in_dim(parts, mine ^ flip, axis, keepdims=False)
        total += lax.ppermute(give, "rows", [(i, i ^ (flip * stride)) for i in range(count)])
    return total


def shards(primal, adjoint, right_vectors, left_vectors, singular):
    count = lax.axis_size("rows")
    sides = lax.axis_size("snap")
    side = lax.axis_index("snap")
    rows, width = primal.shape
    weights = 1.0 / jnp.sqrt(singular)
    norm = 1.0 / jnp.sqrt(jnp.float32(rows * count))
    ring = [(i, (i + 1) % sides) for i in range(sides)]
    cuts = [0, rows * 7 // 8, rows]
    spans = list(zip(cuts[:-1], cuts[1:]))

    def block(matrix, owner):
        return lax.dynamic_slice_in_dim(matrix, owner * width, width, 0)

    group = count // sides
    share = width // group

    near = min(group, 1 << (count.bit_length() - 1) // 2)

    def within(term):
        return exchange(term.reshape(group // near, near, share, width), 1, 1)

    adjoints = [adjoint]
    primals = [[primal[a:b] for a, b in spans]]
    for step in range(1, sides):
        adjoints.append(lax.ppermute(adjoints[-1], "snap", ring))
        primals.append([lax.ppermute(piece, "snap", ring) for piece in primals[-1]])

    terms = [within(inner_cols(adjoint, primal))]
    psi = mul(adjoint, block(left_vectors, side))
    phi = mul(primal, block(right_vectors, side))
    rights = []
    for step in range(1, sides):
        owner = (side - step) % sides
        left = split_matrix(block(left_vectors, owner))
        rights.append(split_matrix(block(right_vectors, owner)))
        theirs, left, rights, terms, psi, phi = lax.optimization_barrier(
            (adjoints[step], left, rights, terms, psi, phi)
        )
        terms.append(within(inner_cols(theirs, primal)))
        psi = add_rows(psi, theirs, left, weights, 0, rows // 2, step == sides - 1)
    blocks = [terms[-t % sides] for t in range(sides)]
    bit = 1
    while bit < sides:
        turn = (side // bit) % 2 == 1
        blocks = [jnp.where(turn, blocks[t - bit], blocks[t]) for t in range(sides)]
        bit *= 2
    total = exchange(jnp.concatenate(blocks), 0, near)
    gram = total * norm
    gram, psi, phi = lax.optimization_barrier((gram, psi, phi))
    for step in range(1, sides):
        for (start, stop), piece in zip(spans, primals[step]):
            last = step == sides - 1
            if start == 0:
                phi = add_rows(phi, piece, rights[step - 1], weights, start, stop // 2, last)
            else:
                phi = end_rows(phi, piece, rights[step - 1], weights, start, last)
    return (gram, phi, psi)


def solution(mesh):
    in_specs = (P("rows", "snap"), P("rows", "snap"), P(None, "snap"), P(None, "snap"), P("snap"))
    out_specs = (P("rows", "snap"), P("rows", "snap"), P("rows", "snap"))
    return jax.shard_map(shards, mesh=mesh, in_specs=in_specs, out_specs=out_specs, check_vma=False)
```

```python
import functools

import jax
import jax.numpy as jnp
from jax import lax
from jax.experimental import pallas as pl
from jax.experimental.pallas import tpu as pltpu
from jax.sharding import PartitionSpec as P

HIGH = lax.Precision.HIGH


def mul(left, right):
    return jnp.dot(left, right, precision=HIGH, preferred_element_type=jnp.float32)


def split(x):
    high = x.astype(jnp.bfloat16)
    return high, (x - high.astype(jnp.float32)).astype(jnp.bfloat16)


def split_kernel(x_ref, high_ref, low_ref):
    high_ref[...], low_ref[...] = split(x_ref[...])


LIMIT = 16 << 20
FREE = pl.CostEstimate(flops=0, bytes_accessed=0, transcendentals=0)


def split_matrix(matrix):
    return pl.pallas_call(
        split_kernel,
        out_shape=[jax.ShapeDtypeStruct(matrix.shape, jnp.bfloat16)] * 2,
        cost_estimate=FREE,
        compiler_params=pltpu.CompilerParams(vmem_limit_bytes=LIMIT),
    )(matrix)


def inner_cols(left, right):
    return lax.dot_general(
        left, right, (((0,), (0,)), ((), ())), precision=HIGH, preferred_element_type=jnp.float32
    )


def add_rows_kernel(last, total_ref, x_ref, high_ref, low_ref, weights_ref, out_ref):
    dot = functools.partial(jnp.dot, preferred_element_type=jnp.float32)
    x_high, x_low = split(x_ref[...])
    total = total_ref[...] + (
        dot(x_high, high_ref[...]) + (dot(x_high, low_ref[...]) + dot(x_low, high_ref[...]))
    )
    out_ref[...] = total * weights_ref[...] if last else total


def add_rows(total, x, matrix, weights, start, tile, last):
    width = total.shape[1]
    depth = x.shape[1]
    first = start // tile
    rows = pl.BlockSpec((tile, width), lambda i: (first + i, 0))
    whole = pl.BlockSpec((depth, width), lambda i: (0, 0))
    return pl.pallas_call(
        functools.partial(add_rows_kernel, last),
        grid=(x.shape[0] // tile,),
        in_specs=[
            rows,
            pl.BlockSpec((tile, depth), lambda i: (i, 0)),
            whole,
            whole,
            pl.BlockSpec((1, width), lambda i: (0, 0)),
        ],
        out_specs=rows,
        out_shape=jax.ShapeDtypeStruct(total.shape, total.dtype),
        input_output_aliases={0: 0},
        cost_estimate=FREE,
        compiler_params=pltpu.CompilerParams(vmem_limit_bytes=LIMIT),
    )(total, x, *matrix, weights[None])


def end_rows_kernel(first, last, total_ref, own_ref, x_ref, high_ref, low_ref, weights_ref, out_ref, held, sem):
    dot = functools.partial(jnp.dot, preferred_element_type=jnp.float32)
    x_high, x_low = split(x_ref[...])
    total = own_ref[...] + (
        dot(x_high, high_ref[...]) + (dot(x_high, low_ref[...]) + dot(x_low, high_ref[...]))
    )
    held[...] = total * weights_ref[...] if last else total
    store = pltpu.make_async_copy(held, out_ref.at[pl.ds(first, x_ref.shape[0])], sem)
    store.start()
    store.wait()


def end_rows(total, own, x, matrix, weights, start, last):
    vmem = pl.BlockSpec(memory_space=pltpu.VMEM)
    apart = pl.BlockSpec(memory_space=pl.ANY)
    return pl.pallas_call(
        functools.partial(end_rows_kernel, start, last),
        in_specs=[apart, vmem, vmem, vmem, vmem, vmem],
        out_specs=apart,
        out_shape=jax.ShapeDtypeStruct(total.shape, total.dtype),
        scratch_shapes=[pltpu.VMEM((x.shape[0], total.shape[1]), jnp.float32), pltpu.SemaphoreType.DMA],
        input_output_aliases={0: 0},
        cost_estimate=FREE,
        compiler_params=pltpu.CompilerParams(vmem_limit_bytes=LIMIT),
    )(total, own, x, *matrix, weights[None])


def exchange(parts, axis, stride):
    count = lax.axis_size("rows")
    digits = parts.shape[axis]
    mine = (lax.axis_index("rows") // stride) % digits
    total = lax.dynamic_index_in_dim(parts, mine, axis, keepdims=False)
    for flip in range(1, digits):
        give = lax.dynamic_index_in_dim(parts, mine ^ flip, axis, keepdims=False)
        total += lax.ppermute(give, "rows", [(i, i ^ (flip * stride)) for i in range(count)])
    return total


def shards(primal, adjoint, right_vectors, left_vectors, singular):
    count = lax.axis_size("rows")
    sides = lax.axis_size("snap")
    side = lax.axis_index("snap")
    rows, width = primal.shape
    weights = 1.0 / jnp.sqrt(singular)
    norm = 1.0 / jnp.sqrt(jnp.float32(rows * count))
    ring = [(i, (i + 1) % sides) for i in range(sides)]
    cuts = [0, rows * 7 // 8, rows]
    spans = list(zip(cuts[:-1], cuts[1:]))

    def block(matrix, owner):
        return lax.dynamic_slice_in_dim(matrix, owner * width, width, 0)

    group = count // sides
    share = width // group

    near = min(group, 1 << (count.bit_length() - 1) // 2)

    def within(term):
        return exchange(term.reshape(group // near, near, share, width), 1, 1)

    adjoints = [adjoint]
    primals = [[primal[a:b] for a, b in spans]]
    for step in range(1, sides):
        adjoints.append(lax.ppermute(adjoints[-1], "snap", ring))
        primals.append([lax.ppermute(piece, "snap", ring) for piece in primals[-1]])

    terms = [within(inner_cols(adjoint, primal))]
    psi = mul(adjoint, block(left_vectors, side))
    phi = mul(primal, block(right_vectors, side))
    rights = []
    for step in range(1, sides):
        owner = (side - step) % sides
        left = split_matrix(block(left_vectors, owner))
        rights.append(split_matrix(block(right_vectors, owner)))
        theirs, left, rights, terms, psi, phi = lax.optimization_barrier(
            (adjoints[step], left, rights, terms, psi, phi)
        )
        terms.append(within(inner_cols(theirs, primal)))
        psi = add_rows(psi, theirs, left, weights, 0, rows // 2, step == sides - 1)
    blocks = [terms[-t % sides] for t in range(sides)]
    bit = 1
    while bit < sides:
        turn = (side // bit) % 2 == 1
        blocks = [jnp.where(turn, blocks[t - bit], blocks[t]) for t in range(sides)]
        bit *= 2
    total = exchange(jnp.concatenate(blocks), 0, near)
    gram = total * norm
    gram, psi, phi = lax.optimization_barrier((gram, psi, phi))
    for step in range(1, sides):
        for (start, stop), piece in zip(spans, primals[step]):
            last = step == sides - 1
            if start == 0:
                own = phi[stop:]
                phi = add_rows(phi, piece, rights[step - 1], weights, start, stop // 2, last)
            else:
                phi = end_rows(phi, own, piece, rights[step - 1], weights, start, last)
    return (gram, phi, psi)


def solution(mesh):
    in_specs = (P("rows", "snap"), P("rows", "snap"), P(None, "snap"), P(None, "snap"), P("snap"))
    out_specs = (P("rows", "snap"), P("rows", "snap"), P("rows", "snap"))
    return jax.shard_map(shards, mesh=mesh, in_specs=in_specs, out_specs=out_specs, check_vma=False)
```

```python
import functools

import jax
import jax.numpy as jnp
from jax import lax
from jax.experimental import pallas as pl
from jax.experimental.pallas import tpu as pltpu
from jax.sharding import PartitionSpec as P

HIGH = lax.Precision.HIGH


def mul(left, right):
    return jnp.dot(left, right, precision=HIGH, preferred_element_type=jnp.float32)


def split(x):
    high = x.astype(jnp.bfloat16)
    return high, (x - high.astype(jnp.float32)).astype(jnp.bfloat16)


def split_kernel(x_ref, high_ref, low_ref):
    high_ref[...], low_ref[...] = split(x_ref[...])


LIMIT = 16 << 20
FREE = pl.CostEstimate(flops=0, bytes_accessed=0, transcendentals=0)
LONG = pl.CostEstimate(flops=6_000_000_000, bytes_accessed=0, transcendentals=0)


def split_matrix(matrix, cost=FREE):
    return pl.pallas_call(
        split_kernel,
        out_shape=[jax.ShapeDtypeStruct(matrix.shape, jnp.bfloat16)] * 2,
        cost_estimate=cost,
        compiler_params=pltpu.CompilerParams(vmem_limit_bytes=LIMIT),
    )(matrix)


def inner_cols(left, right):
    return lax.dot_general(
        left, right, (((0,), (0,)), ((), ())), precision=HIGH, preferred_element_type=jnp.float32
    )


def add_rows_kernel(last, total_ref, x_ref, high_ref, low_ref, weights_ref, out_ref):
    dot = functools.partial(jnp.dot, preferred_element_type=jnp.float32)
    x_high, x_low = split(x_ref[...])
    total = total_ref[...] + (
        dot(x_high, high_ref[...]) + (dot(x_high, low_ref[...]) + dot(x_low, high_ref[...]))
    )
    out_ref[...] = total * weights_ref[...] if last else total


def add_rows(total, x, matrix, weights, start, tile, last):
    width = total.shape[1]
    depth = x.shape[1]
    first = start // tile
    rows = pl.BlockSpec((tile, width), lambda i: (first + i, 0))
    whole = pl.BlockSpec((depth, width), lambda i: (0, 0))
    return pl.pallas_call(
        functools.partial(add_rows_kernel, last),
        grid=(x.shape[0] // tile,),
        in_specs=[
            rows,
            pl.BlockSpec((tile, depth), lambda i: (i, 0)),
            whole,
            whole,
            pl.BlockSpec((1, width), lambda i: (0, 0)),
        ],
        out_specs=rows,
        out_shape=jax.ShapeDtypeStruct(total.shape, total.dtype),
        input_output_aliases={0: 0},
        cost_estimate=FREE,
        compiler_params=pltpu.CompilerParams(vmem_limit_bytes=LIMIT),
    )(total, x, *matrix, weights[None])


def end_rows_kernel(total_ref, own_ref, *refs):
    *x_refs, high_ref, low_ref, weights_ref, out_ref, held, sem = refs
    dot = functools.partial(jnp.dot, preferred_element_type=jnp.float32)
    rows = held.shape[0]
    x_high, x_low = split(jnp.concatenate([x_ref[...] for x_ref in x_refs]))
    total = own_ref[...] + (
        dot(x_high, high_ref[...]) + (dot(x_high, low_ref[...]) + dot(x_low, high_ref[...]))
    )
    held[...] = total * weights_ref[...]
    store = pltpu.make_async_copy(held, out_ref.at[pl.ds(out_ref.shape[0] - rows, rows)], sem)
    store.start()
    store.wait()


def end_rows(total, own, xs, matrix, weights):
    vmem = pl.BlockSpec(memory_space=pltpu.VMEM)
    apart = pl.BlockSpec(memory_space=pl.ANY)
    return pl.pallas_call(
        end_rows_kernel,
        in_specs=[apart] + [vmem] * (4 + len(xs)),
        out_specs=apart,
        out_shape=jax.ShapeDtypeStruct(total.shape, total.dtype),
        scratch_shapes=[pltpu.VMEM(own.shape, jnp.float32), pltpu.SemaphoreType.DMA],
        input_output_aliases={0: 0},
        cost_estimate=FREE,
        compiler_params=pltpu.CompilerParams(vmem_limit_bytes=LIMIT),
    )(total, own, *xs, *matrix, weights[None])


def swap(x):
    return lax.ppermute(x, "rows", [(i, i ^ 1) for i in range(lax.axis_size("rows"))])


def pass_on(x, parity):
    count = lax.axis_size("rows")
    sides = lax.axis_size("snap")
    pairs = [
        (row * sides + side, row * sides + (side + 1) % sides)
        for row in range(parity, count, 2)
        for side in range(sides)
    ]
    return lax.ppermute(x, ("rows", "snap"), pairs)


def exchange(parts, axis, stride):
    count = lax.axis_size("rows")
    digits = parts.shape[axis]
    mine = (lax.axis_index("rows") // stride) % digits
    total = lax.dynamic_index_in_dim(parts, mine, axis, keepdims=False)
    for flip in range(1, digits):
        give = lax.dynamic_index_in_dim(parts, mine ^ flip, axis, keepdims=False)
        total += lax.ppermute(give, "rows", [(i, i ^ (flip * stride)) for i in range(count)])
    return total


def shards(primal, adjoint, right_vectors, left_vectors, singular):
    count = lax.axis_size("rows")
    sides = lax.axis_size("snap")
    side = lax.axis_index("snap")
    rows, width = primal.shape
    weights = 1.0 / jnp.sqrt(singular)
    norm = 1.0 / jnp.sqrt(jnp.float32(rows * count))
    ring = [(i, (i + 1) % sides) for i in range(sides)]
    cuts = [0, rows * 27 // 32, rows * 28 // 32, rows]
    spans = list(zip(cuts[:-1], cuts[1:]))

    def block(matrix, owner):
        return lax.dynamic_slice_in_dim(matrix, owner * width, width, 0)

    group = count // sides
    share = width // group

    near = min(group, 1 << (count.bit_length() - 1) // 2)

    def within(term):
        return exchange(term.reshape(group // near, near, share, width), 1, 1)

    adjoints = [adjoint]
    primals = [[primal[a:b] for a, b in spans]]
    for step in range(1, sides - 1):
        primals.append([lax.ppermute(piece, "snap", ring) for piece in primals[-1]])
    most, few, end = primals[-1]
    odd = lax.axis_index("rows") % 2 == 1
    terms = [within(inner_cols(adjoint, primal))]
    both, most, terms = lax.optimization_barrier(
        (jnp.concatenate([few, swap(few)]), most, terms)
    )
    extra = pass_on(both, 1)
    most, end = lax.ppermute(most, "snap", ring), lax.ppermute(end, "snap", ring)
    psi = mul(adjoint, block(left_vectors, side))
    phi = mul(primal, block(right_vectors, side))
    rights = []
    for step in range(1, sides):
        owner = (side - step) % sides
        left = block(left_vectors, owner)
        if step == 1:
            left, extra = lax.optimization_barrier((left, extra))
            left = split_matrix(left, LONG)
        else:
            left = split_matrix(left)
        rights.append(split_matrix(block(right_vectors, owner)))
        adjoints.append(lax.ppermute(adjoints[-1], "snap", ring))
        theirs, left, rights, terms, psi, phi = lax.optimization_barrier(
            (adjoints[step], left, rights, terms, psi, phi)
        )
        terms.append(within(inner_cols(theirs, primal)))
        psi = add_rows(psi, theirs, left, weights, 0, rows // 2, step == sides - 1)
    back = swap(extra[few.shape[0] :])
    few = jnp.where(odd, extra[: few.shape[0]], back)
    for step in range(1, sides - 1):
        for (start, stop), piece in zip(spans, primals[step]):
            phi = add_rows(phi, piece, rights[step - 1], weights, start, stop - start, False)
    phi = add_rows(phi, few, rights[-1], weights, cuts[1], len(few), True)
    own = phi[cuts[2] :]
    blocks = [terms[-t % sides] for t in range(sides)]
    bit = 1
    while bit < sides:
        turn = (side // bit) % 2 == 1
        blocks = [jnp.where(turn, blocks[t - bit], blocks[t]) for t in range(sides)]
        bit *= 2
    total = exchange(jnp.concatenate(blocks), 0, near)
    gram = total * norm
    gram, psi, phi, own = lax.optimization_barrier((gram, psi, phi, own))
    phi = add_rows(phi, most, rights[-1], weights, 0, cuts[1] // 2, True)
    phi = end_rows(phi, own, [end], rights[-1], weights)
    return (gram, phi, psi)


def solution(mesh):
    in_specs = (P("rows", "snap"), P("rows", "snap"), P(None, "snap"), P(None, "snap"), P("snap"))
    out_specs = (P("rows", "snap"), P("rows", "snap"), P("rows", "snap"))
    return jax.shard_map(shards, mesh=mesh, in_specs=in_specs, out_specs=out_specs, check_vma=False)
```

```python
import functools
import math

import jax
import jax.numpy as jnp
from jax import lax
from jax.experimental import pallas as pl
from jax.experimental.pallas import tpu as pltpu
from jax.sharding import PartitionSpec as P

HIGH = lax.Precision.HIGH


def mul(left, right):
    return jnp.dot(left, right, precision=HIGH, preferred_element_type=jnp.float32)


def split(x):
    high = x.astype(jnp.bfloat16)
    return high, (x - high.astype(jnp.float32)).astype(jnp.bfloat16)


def split_kernel(x_ref, high_ref, low_ref):
    high_ref[...], low_ref[...] = split(x_ref[...])


LIMIT = 16 << 20
FREE = pl.CostEstimate(flops=0, bytes_accessed=0, transcendentals=0)
LONG = pl.CostEstimate(flops=6_000_000_000, bytes_accessed=0, transcendentals=0)


def split_matrix(matrix, cost=FREE):
    return pl.pallas_call(
        split_kernel,
        out_shape=[jax.ShapeDtypeStruct(matrix.shape, jnp.bfloat16)] * 2,
        cost_estimate=cost,
        compiler_params=pltpu.CompilerParams(vmem_limit_bytes=LIMIT),
    )(matrix)


def inner_cols(left, right):
    return lax.dot_general(
        left, right, (((0,), (0,)), ((), ())), precision=HIGH, preferred_element_type=jnp.float32
    )


def add_rows_kernel(last, total_ref, x_ref, high_ref, low_ref, weights_ref, out_ref):
    dot = functools.partial(jnp.dot, preferred_element_type=jnp.float32)
    x_high, x_low = split(x_ref[...])
    total = total_ref[...] + (
        dot(x_high, high_ref[...]) + (dot(x_high, low_ref[...]) + dot(x_low, high_ref[...]))
    )
    out_ref[...] = total * weights_ref[...] if last else total


def add_rows(total, x, matrix, weights, start, tile, last):
    width = total.shape[1]
    depth = x.shape[1]
    first = start // tile
    rows = pl.BlockSpec((tile, width), lambda i: (first + i, 0))
    whole = pl.BlockSpec((depth, width), lambda i: (0, 0))
    return pl.pallas_call(
        functools.partial(add_rows_kernel, last),
        grid=(x.shape[0] // tile,),
        in_specs=[
            rows,
            pl.BlockSpec((tile, depth), lambda i: (i, 0)),
            whole,
            whole,
            pl.BlockSpec((1, width), lambda i: (0, 0)),
        ],
        out_specs=rows,
        out_shape=jax.ShapeDtypeStruct(total.shape, total.dtype),
        input_output_aliases={0: 0},
        cost_estimate=FREE,
        compiler_params=pltpu.CompilerParams(vmem_limit_bytes=LIMIT),
    )(total, x, *matrix, weights[None])


def end_rows_kernel(first, total_ref, own_ref, x_ref, high_ref, low_ref, weights_ref, out_ref, held, sem):
    dot = functools.partial(jnp.dot, preferred_element_type=jnp.float32)
    rows = held.shape[0]
    x_high, x_low = split(x_ref[...])
    by_high = dot(jnp.concatenate([x_high, x_low]), high_ref[...])
    total = own_ref[...] + (by_high[:rows] + (dot(x_high, low_ref[...]) + by_high[rows:]))
    held[...] = total * weights_ref[...]
    store = pltpu.make_async_copy(held, out_ref.at[pl.ds(first, rows)], sem)
    store.start()
    store.wait()


def end_rows(total, own, x, matrix, weights, first):
    vmem = pl.BlockSpec(memory_space=pltpu.VMEM)
    apart = pl.BlockSpec(memory_space=pl.ANY)
    return pl.pallas_call(
        functools.partial(end_rows_kernel, first),
        in_specs=[apart] + [vmem] * 5,
        out_specs=apart,
        out_shape=jax.ShapeDtypeStruct(total.shape, total.dtype),
        scratch_shapes=[pltpu.VMEM(own.shape, jnp.float32), pltpu.SemaphoreType.DMA],
        input_output_aliases={0: 0},
        cost_estimate=FREE,
        compiler_params=pltpu.CompilerParams(vmem_limit_bytes=LIMIT),
    )(total, own, x, *matrix, weights[None])


def swap(x):
    return lax.ppermute(x, "rows", [(i, i ^ 1) for i in range(lax.axis_size("rows"))])


def pass_on(x, parity):
    count = lax.axis_size("rows")
    sides = lax.axis_size("snap")
    pairs = [
        (row * sides + side, row * sides + (side + 1) % sides)
        for row in range(parity, count, 2)
        for side in range(sides)
    ]
    return lax.ppermute(x, ("rows", "snap"), pairs)


def exchange(parts, axis, stride, beside=None):
    count = lax.axis_size("rows")
    digits = parts.shape[axis]
    mine = (lax.axis_index("rows") // stride) % digits
    arrived = []
    for flip in range(1, digits):
        give = lax.dynamic_index_in_dim(parts, mine ^ flip, axis, keepdims=False)
        pairs = [(i, i ^ (flip * stride)) for i in range(count)]
        arrived.append(lax.ppermute(give, "rows", pairs))
    if beside is not None:
        arrived, beside = lax.optimization_barrier((arrived, beside))
    return sum(arrived, lax.dynamic_index_in_dim(parts, mine, axis, keepdims=False)), beside


def shards(primal, adjoint, right_vectors, left_vectors, singular):
    count = lax.axis_size("rows")
    sides = lax.axis_size("snap")
    side = lax.axis_index("snap")
    rows, width = primal.shape
    weights = 1.0 / jnp.sqrt(singular)
    norm = 1.0 / jnp.sqrt(jnp.float32(rows * count))
    ring = [(i, (i + 1) % sides) for i in range(sides)]
    cuts = [0, rows * 27 // 32, rows * 28 // 32, rows]
    spans = list(zip(cuts[:-1], cuts[1:]))

    def block(matrix, owner):
        return lax.dynamic_slice_in_dim(matrix, owner * width, width, 0)

    group = count // sides
    share = width // group

    near = min(group, 1 << (count.bit_length() - 1) // 2)

    def within(term, beside=None):
        return exchange(term.reshape(group // near, near, share, width), 1, 1, beside)

    adjoints = [adjoint]
    primals = [[primal[a:b] for a, b in spans]]
    for step in range(1, sides - 1):
        primals.append([lax.ppermute(piece, "snap", ring) for piece in primals[-1]])
    most, few, end = primals[-1]
    odd = lax.axis_index("rows") % 2 == 1
    terms = [within(inner_cols(adjoint, primal))[0]]
    both, most, terms = lax.optimization_barrier(
        (jnp.concatenate([few, swap(few)]), most, terms)
    )
    extra = pass_on(both, 1)
    most, end = [lax.ppermute(piece, "snap", ring) for piece in (most, end)]
    psi = mul(adjoint, block(left_vectors, side))
    phi = mul(primal, block(right_vectors, side))
    rights = []
    for step in range(1, sides):
        owner = (side - step) % sides
        left = block(left_vectors, owner)
        if step == 1:
            left, extra = lax.optimization_barrier((left, extra))
            left = split_matrix(left, LONG)
        else:
            left = split_matrix(left)
        rights.append(split_matrix(block(right_vectors, owner)))
        adjoints.append(lax.ppermute(adjoints[-1], "snap", ring))
        theirs, left, rights, terms, psi, phi = lax.optimization_barrier(
            (adjoints[step], left, rights, terms, psi, phi)
        )
        psi = add_rows(psi, theirs, left, weights, 0, rows // 2, step == sides - 1)
        term, psi = within(inner_cols(theirs, primal), psi)
        terms.append(term)
    back = swap(extra[few.shape[0] :])
    few = jnp.where(odd, extra[: few.shape[0]], back)
    for step in range(1, sides - 1):
        for (start, stop), piece in zip(spans, primals[step]):
            tile = math.gcd(start, stop - start)
            phi = add_rows(phi, piece, rights[step - 1], weights, start, tile, False)
    phi = add_rows(phi, few, rights[-1], weights, cuts[1], len(few), True)
    own = phi[cuts[2] :]
    blocks = [terms[-t % sides] for t in range(sides)]
    bit = 1
    while bit < sides:
        turn = (side // bit) % 2 == 1
        blocks = [jnp.where(turn, blocks[t - bit], blocks[t]) for t in range(sides)]
        bit *= 2
    total, (phi, own) = exchange(jnp.concatenate(blocks), 0, near, (phi, own))
    gram = total * norm
    gram, psi, phi, own = lax.optimization_barrier((gram, psi, phi, own))
    phi = add_rows(phi, most, rights[-1], weights, 0, cuts[1] // 2, True)
    phi = end_rows(phi, own, end, rights[-1], weights, cuts[2])
    return (gram, phi, psi)


def solution(mesh):
    in_specs = (P("rows", "snap"), P("rows", "snap"), P(None, "snap"), P(None, "snap"), P("snap"))
    out_specs = (P("rows", "snap"), P("rows", "snap"), P("rows", "snap"))
    return jax.shard_map(shards, mesh=mesh, in_specs=in_specs, out_specs=out_specs, check_vma=False)
```

```python
import functools
import math

import jax
import jax.numpy as jnp
from jax import lax
from jax.experimental import pallas as pl
from jax.experimental.pallas import tpu as pltpu
from jax.sharding import PartitionSpec as P

HIGH = lax.Precision.HIGH


def mul(left, right):
    return jnp.dot(left, right, precision=HIGH, preferred_element_type=jnp.float32)


def split(x):
    high = x.astype(jnp.bfloat16)
    return high, (x - high.astype(jnp.float32)).astype(jnp.bfloat16)


def split_kernel(x_ref, high_ref, low_ref):
    high_ref[...], low_ref[...] = split(x_ref[...])


LIMIT = 16 << 20
FREE = pl.CostEstimate(flops=0, bytes_accessed=0, transcendentals=0)
LONG = pl.CostEstimate(flops=6_000_000_000, bytes_accessed=0, transcendentals=0)


def split_matrix(matrix, cost=FREE):
    return pl.pallas_call(
        split_kernel,
        out_shape=[jax.ShapeDtypeStruct(matrix.shape, jnp.bfloat16)] * 2,
        cost_estimate=cost,
        compiler_params=pltpu.CompilerParams(vmem_limit_bytes=LIMIT),
    )(matrix)


def inner_cols(left, right):
    return lax.dot_general(
        left, right, (((0,), (0,)), ((), ())), precision=HIGH, preferred_element_type=jnp.float32
    )


def add_rows_kernel(last, total_ref, x_ref, high_ref, low_ref, weights_ref, out_ref):
    dot = functools.partial(jnp.dot, preferred_element_type=jnp.float32)
    x_high, x_low = split(x_ref[...])
    total = total_ref[...] + (
        dot(x_high, high_ref[...]) + (dot(x_high, low_ref[...]) + dot(x_low, high_ref[...]))
    )
    out_ref[...] = total * weights_ref[...] if last else total


def add_rows(total, x, matrix, weights, start, tile, last):
    width = total.shape[1]
    depth = x.shape[1]
    first = start // tile
    rows = pl.BlockSpec((tile, width), lambda i: (first + i, 0))
    whole = pl.BlockSpec((depth, width), lambda i: (0, 0))
    return pl.pallas_call(
        functools.partial(add_rows_kernel, last),
        grid=(x.shape[0] // tile,),
        in_specs=[
            rows,
            pl.BlockSpec((tile, depth), lambda i: (i, 0)),
            whole,
            whole,
            pl.BlockSpec((1, width), lambda i: (0, 0)),
        ],
        out_specs=rows,
        out_shape=jax.ShapeDtypeStruct(total.shape, total.dtype),
        input_output_aliases={0: 0},
        cost_estimate=FREE,
        compiler_params=pltpu.CompilerParams(vmem_limit_bytes=LIMIT),
    )(total, x, *matrix, weights[None])


def end_rows_kernel(first, total_ref, own_ref, x_ref, high_ref, low_ref, weights_ref, out_ref, held, sem):
    dot = functools.partial(jnp.dot, preferred_element_type=jnp.float32)
    rows = held.shape[0]
    x_high, x_low = split(x_ref[...])
    by_high = dot(jnp.concatenate([x_high, x_low]), high_ref[...])
    total = own_ref[...] + (by_high[:rows] + (dot(x_high, low_ref[...]) + by_high[rows:]))
    held[...] = total * weights_ref[...]
    store = pltpu.make_async_copy(held, out_ref.at[pl.ds(first, rows)], sem)
    store.start()
    store.wait()


def end_rows(total, own, x, matrix, weights, first):
    vmem = pl.BlockSpec(memory_space=pltpu.VMEM)
    apart = pl.BlockSpec(memory_space=pl.ANY)
    return pl.pallas_call(
        functools.partial(end_rows_kernel, first),
        in_specs=[apart] + [vmem] * 5,
        out_specs=apart,
        out_shape=jax.ShapeDtypeStruct(total.shape, total.dtype),
        scratch_shapes=[pltpu.VMEM(own.shape, jnp.float32), pltpu.SemaphoreType.DMA],
        input_output_aliases={0: 0},
        cost_estimate=FREE,
        compiler_params=pltpu.CompilerParams(vmem_limit_bytes=LIMIT),
    )(total, own, x, *matrix, weights[None])


def swap(x):
    return lax.ppermute(x, "rows", [(i, i ^ 1) for i in range(lax.axis_size("rows"))])


def pass_on(x, parity):
    count = lax.axis_size("rows")
    sides = lax.axis_size("snap")
    pairs = [
        (row * sides + side, row * sides + (side + 1) % sides)
        for row in range(parity, count, 2)
        for side in range(sides)
    ]
    return lax.ppermute(x, ("rows", "snap"), pairs)


def exchange(parts, axis, stride, beside=None):
    count = lax.axis_size("rows")
    digits = parts.shape[axis]
    mine = (lax.axis_index("rows") // stride) % digits
    arrived = []
    for flip in range(1, digits):
        give = lax.dynamic_index_in_dim(parts, mine ^ flip, axis, keepdims=False)
        pairs = [(i, i ^ (flip * stride)) for i in range(count)]
        arrived.append(lax.ppermute(give, "rows", pairs))
    if beside is not None:
        arrived, beside = lax.optimization_barrier((arrived, beside))
    return sum(arrived, lax.dynamic_index_in_dim(parts, mine, axis, keepdims=False)), beside


def shards(primal, adjoint, right_vectors, left_vectors, singular):
    count = lax.axis_size("rows")
    sides = lax.axis_size("snap")
    side = lax.axis_index("snap")
    rows, width = primal.shape
    weights = 1.0 / jnp.sqrt(singular)
    norm = 1.0 / jnp.sqrt(jnp.float32(rows * count))
    ring = [(i, (i + 1) % sides) for i in range(sides)]
    cuts = [0, rows * 27 // 32, rows * 28 // 32, rows]
    spans = list(zip(cuts[:-1], cuts[1:]))

    def block(matrix, owner):
        return lax.dynamic_slice_in_dim(matrix, owner * width, width, 0)

    group = count // sides
    share = width // group

    near = min(group, 1 << (count.bit_length() - 1) // 2)

    def within(term, beside=None):
        return exchange(term.reshape(group // near, near, share, width), 1, 1, beside)

    adjoints = [adjoint]
    primals = [[primal[a:b] for a, b in spans]]
    for step in range(1, sides - 1):
        primals.append([lax.ppermute(piece, "snap", ring) for piece in primals[-1]])
    most, few, end = primals[-1]
    odd = lax.axis_index("rows") % 2 == 1
    terms = [within(inner_cols(adjoint, primal))[0]]
    both, most, terms = lax.optimization_barrier(
        (jnp.concatenate([few, swap(few)]), most, terms)
    )
    extra = pass_on(both, 1)
    most, end = [lax.ppermute(piece, "snap", ring) for piece in (most, end)]
    psi = mul(adjoint, block(left_vectors, side))
    phi = mul(primal, block(right_vectors, side))
    rights = []
    for step in range(1, sides):
        owner = (side - step) % sides
        left = block(left_vectors, owner)
        if step == 1:
            left, extra = lax.optimization_barrier((left, extra))
            left = split_matrix(left, LONG)
        else:
            left = split_matrix(left)
        rights.append(split_matrix(block(right_vectors, owner)))
        adjoints.append(lax.ppermute(adjoints[-1], "snap", ring))
        theirs, left, rights, terms, psi, phi = lax.optimization_barrier(
            (adjoints[step], left, rights, terms, psi, phi)
        )
        psi = add_rows(psi, theirs, left, weights, 0, rows // 2, step == sides - 1)
        term, psi = within(inner_cols(theirs, primal), psi)
        terms.append(term)
    back = swap(extra[few.shape[0] :])
    few = jnp.where(odd, extra[: few.shape[0]], back)
    for step in range(1, sides - 1):
        for (start, stop), piece in zip(spans, primals[step]):
            tile = math.gcd(start, stop - start)
            phi = add_rows(phi, piece, rights[step - 1], weights, start, tile, False)
    phi = add_rows(phi, few, rights[-1], weights, cuts[1], len(few), True)
    own = phi[cuts[2] :]
    blocks = [terms[-t % sides] for t in range(sides)]
    bit = 1
    while bit < sides:
        turn = (side // bit) % 2 == 1
        blocks = [jnp.where(turn, blocks[t - bit], blocks[t]) for t in range(sides)]
        bit *= 2
    total, (phi, own) = exchange(jnp.concatenate(blocks), 0, near, (phi, own))
    gram = total * norm
    gram, psi, phi, own = lax.optimization_barrier((gram, psi, phi, own))
    phi = add_rows(phi, most, rights[-1], weights, 0, cuts[1] // 3, True)
    phi = end_rows(phi, own, end, rights[-1], weights, cuts[2])
    return (gram, phi, psi)


def solution(mesh):
    in_specs = (P("rows", "snap"), P("rows", "snap"), P(None, "snap"), P(None, "snap"), P("snap"))
    out_specs = (P("rows", "snap"), P("rows", "snap"), P("rows", "snap"))
    return jax.shard_map(shards, mesh=mesh, in_specs=in_specs, out_specs=out_specs, check_vma=False)
```

```python
import functools
import math

import jax
import jax.numpy as jnp
from jax import lax
from jax.experimental import pallas as pl
from jax.experimental.pallas import tpu as pltpu
from jax.sharding import PartitionSpec as P

HIGH = lax.Precision.HIGH


def mul(left, right):
    return jnp.dot(left, right, precision=HIGH, preferred_element_type=jnp.float32)


def split(x):
    high = x.astype(jnp.bfloat16)
    return high, (x - high.astype(jnp.float32)).astype(jnp.bfloat16)


def split_kernel(x_ref, high_ref, low_ref):
    high_ref[...], low_ref[...] = split(x_ref[...])


LIMIT = 16 << 20
FREE = pl.CostEstimate(flops=0, bytes_accessed=0, transcendentals=0)
LONG = pl.CostEstimate(flops=6_000_000_000, bytes_accessed=0, transcendentals=0)


def split_matrix(matrix, cost=FREE):
    return pl.pallas_call(
        split_kernel,
        out_shape=[jax.ShapeDtypeStruct(matrix.shape, jnp.bfloat16)] * 2,
        cost_estimate=cost,
        compiler_params=pltpu.CompilerParams(vmem_limit_bytes=LIMIT),
    )(matrix)


def inner_cols(left, right):
    return lax.dot_general(
        left, right, (((0,), (0,)), ((), ())), precision=HIGH, preferred_element_type=jnp.float32
    )


def add_rows_kernel(last, total_ref, x_ref, high_ref, low_ref, weights_ref, out_ref):
    dot = functools.partial(jnp.dot, preferred_element_type=jnp.float32)
    x_high, x_low = split(x_ref[...])
    total = total_ref[...] + (
        dot(x_high, high_ref[...]) + (dot(x_high, low_ref[...]) + dot(x_low, high_ref[...]))
    )
    out_ref[...] = total * weights_ref[...] if last else total


def add_rows(total, x, matrix, weights, start, tile, last):
    width = total.shape[1]
    depth = x.shape[1]
    first = start // tile
    rows = pl.BlockSpec((tile, width), lambda i: (first + i, 0))
    whole = pl.BlockSpec((depth, width), lambda i: (0, 0))
    return pl.pallas_call(
        functools.partial(add_rows_kernel, last),
        grid=(x.shape[0] // tile,),
        in_specs=[
            rows,
            pl.BlockSpec((tile, depth), lambda i: (i, 0)),
            whole,
            whole,
            pl.BlockSpec((1, width), lambda i: (0, 0)),
        ],
        out_specs=rows,
        out_shape=jax.ShapeDtypeStruct(total.shape, total.dtype),
        input_output_aliases={0: 0},
        cost_estimate=FREE,
        compiler_params=pltpu.CompilerParams(vmem_limit_bytes=LIMIT),
    )(total, x, *matrix, weights[None])


def end_rows_kernel(first, total_ref, own_ref, x_ref, high_ref, low_ref, weights_ref, out_ref, held, sem):
    dot = functools.partial(jnp.dot, preferred_element_type=jnp.float32)
    rows = held.shape[0]
    x_high, x_low = split(x_ref[...])
    by_high = dot(jnp.concatenate([x_high, x_low]), high_ref[...])
    total = own_ref[...] + (by_high[:rows] + (dot(x_high, low_ref[...]) + by_high[rows:]))
    held[...] = total * weights_ref[...]
    store = pltpu.make_async_copy(held, out_ref.at[pl.ds(first, rows)], sem)
    store.start()
    store.wait()


def end_rows(total, own, x, matrix, weights, first):
    vmem = pl.BlockSpec(memory_space=pltpu.VMEM)
    apart = pl.BlockSpec(memory_space=pl.ANY)
    return pl.pallas_call(
        functools.partial(end_rows_kernel, first),
        in_specs=[apart] + [vmem] * 5,
        out_specs=apart,
        out_shape=jax.ShapeDtypeStruct(total.shape, total.dtype),
        scratch_shapes=[pltpu.VMEM(own.shape, jnp.float32), pltpu.SemaphoreType.DMA],
        input_output_aliases={0: 0},
        cost_estimate=FREE,
        compiler_params=pltpu.CompilerParams(vmem_limit_bytes=LIMIT),
    )(total, own, x, *matrix, weights[None])


def swap(x):
    return lax.ppermute(x, "rows", [(i, i ^ 1) for i in range(lax.axis_size("rows"))])


def pass_on(x, parity):
    count = lax.axis_size("rows")
    sides = lax.axis_size("snap")
    pairs = [
        (row * sides + side, row * sides + (side + 1) % sides)
        for row in range(parity, count, 2)
        for side in range(sides)
    ]
    return lax.ppermute(x, ("rows", "snap"), pairs)


def exchange(parts, axis, stride, beside=None):
    count = lax.axis_size("rows")
    digits = parts.shape[axis]
    mine = (lax.axis_index("rows") // stride) % digits
    arrived = []
    for flip in range(1, digits):
        give = lax.dynamic_index_in_dim(parts, mine ^ flip, axis, keepdims=False)
        pairs = [(i, i ^ (flip * stride)) for i in range(count)]
        arrived.append(lax.ppermute(give, "rows", pairs))
    if beside is not None:
        arrived, beside = lax.optimization_barrier((arrived, beside))
    return sum(arrived, lax.dynamic_index_in_dim(parts, mine, axis, keepdims=False)), beside


def shards(primal, adjoint, right_vectors, left_vectors, singular):
    count = lax.axis_size("rows")
    sides = lax.axis_size("snap")
    side = lax.axis_index("snap")
    rows, width = primal.shape
    weights = 1.0 / jnp.sqrt(singular)
    norm = 1.0 / jnp.sqrt(jnp.float32(rows * count))
    ring = [(i, (i + 1) % sides) for i in range(sides)]
    cuts = [0, rows * 26 // 32, rows * 27 // 32, rows]
    spans = list(zip(cuts[:-1], cuts[1:]))

    def block(matrix, owner):
        return lax.dynamic_slice_in_dim(matrix, owner * width, width, 0)

    group = count // sides
    share = width // group

    near = min(group, 1 << (count.bit_length() - 1) // 2)

    def within(term, beside=None):
        return exchange(term.reshape(group // near, near, share, width), 1, 1, beside)

    adjoints = [adjoint]
    primals = [[primal[a:b] for a, b in spans]]
    for step in range(1, sides - 1):
        primals.append([lax.ppermute(piece, "snap", ring) for piece in primals[-1]])
    most, few, end = primals[-1]
    odd = lax.axis_index("rows") % 2 == 1
    terms = [within(inner_cols(adjoint, primal))[0]]
    both, most, terms = lax.optimization_barrier(
        (jnp.concatenate([few, swap(few)]), most, terms)
    )
    extra = pass_on(both, 1)
    most, end = [lax.ppermute(piece, "snap", ring) for piece in (most, end)]
    psi = mul(adjoint, block(left_vectors, side))
    phi = mul(primal, block(right_vectors, side))
    rights = []
    for step in range(1, sides):
        owner = (side - step) % sides
        left = block(left_vectors, owner)
        if step == 1:
            left, extra = lax.optimization_barrier((left, extra))
            left = split_matrix(left, LONG)
        else:
            left = split_matrix(left)
        rights.append(split_matrix(block(right_vectors, owner)))
        adjoints.append(lax.ppermute(adjoints[-1], "snap", ring))
        theirs, left, rights, terms, psi, phi = lax.optimization_barrier(
            (adjoints[step], left, rights, terms, psi, phi)
        )
        psi = add_rows(psi, theirs, left, weights, 0, rows // 2, step == sides - 1)
        term, psi = within(inner_cols(theirs, primal), psi)
        terms.append(term)
    back = swap(extra[few.shape[0] :])
    few = jnp.where(odd, extra[: few.shape[0]], back)
    for step in range(1, sides - 1):
        for (start, stop), piece in zip(spans, primals[step]):
            tile = math.gcd(start, stop - start)
            phi = add_rows(phi, piece, rights[step - 1], weights, start, tile, False)
    phi = add_rows(phi, few, rights[-1], weights, cuts[1], len(few), True)
    own = phi[cuts[2] :]
    blocks = [terms[-t % sides] for t in range(sides)]
    bit = 1
    while bit < sides:
        turn = (side // bit) % 2 == 1
        blocks = [jnp.where(turn, blocks[t - bit], blocks[t]) for t in range(sides)]
        bit *= 2
    total, (phi, own) = exchange(jnp.concatenate(blocks), 0, near, (phi, own))
    gram = total * norm
    gram, psi, phi, own = lax.optimization_barrier((gram, psi, phi, own))
    phi = add_rows(phi, most, rights[-1], weights, 0, cuts[1] // 2, True)
    phi = end_rows(phi, own, end, rights[-1], weights, cuts[2])
    return (gram, phi, psi)


def solution(mesh):
    in_specs = (P("rows", "snap"), P("rows", "snap"), P(None, "snap"), P(None, "snap"), P("snap"))
    out_specs = (P("rows", "snap"), P("rows", "snap"), P("rows", "snap"))
    return jax.shard_map(shards, mesh=mesh, in_specs=in_specs, out_specs=out_specs, check_vma=False)
```
